256 devices in a mesh: dp: 128 (over z, y, x), tensor: 2 (over core).
Axes of the slice: x: 4, y: 4, z: 8, core: 2. Of those that a mesh axis runs over, the one named last changes fastest.
Arguments:
- inputs: bfloat16 [32768, 4096], P('dp', 'tensor'), may hold values from -1200 to 1200
- out_grad: bfloat16 [32768, 4096], P(('dp', 'tensor')), may hold values from -6 to 6
- w_frozen: bfloat16 [4096, 4096], P('tensor'), may hold values from -0.09375 to 0.09375
- adapter_down: bfloat16 [4096, 1024], P('tensor'), may hold values from -0.125 to 0.125
- adapter_up: bfloat16 [1024, 4096], P('tensor'), may hold values from -0.09375 to 0.09375
Outputs:
- input_grad: bfloat16 [32768, 4096], P('dp', 'tensor')
- down_update: bfloat16 [4096, 1024], P('tensor')
- up_update: bfloat16 [1024, 4096], P('tensor')
The draws below stay inside these ranges and needn't reach their ends.
All inputs are finite; a program needn't handle non-finite values.
Results may differ from the reference program's by a relative error of at most 0.0051.
Values may be sent and summed in bfloat16 or wider, within the bound.
No kernel may reach another device: no remote copies, remote signals or barrier semaphores. Data moves between devices by JAX's collectives and lax.ppermute only.
A program may use at most 192 MiB of HBM per device.

```python
import math
import jax
import jax.numpy as jnp

D_IN = 4096
D_OUT = 4096
RANK = 1024
TOKENS = 32768


def draw_inputs(key, part):
    key = jax.random.fold_in(key, 11)
    first, second = jax.random.split(key, 2)
    ramp = 1.0 + 2.0 * jnp.arange(D_IN, dtype=jnp.float32) / D_IN
    column_scale = jnp.exp(jax.random.uniform(first, (D_IN,), jnp.float32, 0.0, math.log(10.0))) * ramp
    values = jnp.clip(jax.random.normal(second, (TOKENS, D_IN), jnp.float32), -4.0, 4.0)
    return (values * column_scale[None, :]).astype(jnp.bfloat16)


def with_spikes(values, own_key, source, target, blocks, factor):
    def block_of(axis_at):
        return (jnp.arange(values.shape[axis_at]) // (values.shape[axis_at] // blocks)).reshape((-1,) + (1,) * (values.ndim - 1 - axis_at))

    first = jax.random.permutation(own_key, blocks)[block_of(target)]
    far = (block_of(target) + blocks // 2) % blocks
    return jnp.where((block_of(source) == first) | (block_of(source) == far), factor * values, values)


def steps_of(rng, dims, shards, low, top_value):
    factor_of, own = 1.0, jax.random.fold_in(rng, 6)
    for position, shards_of in shards:
        steps = jnp.exp(jax.random.uniform(jax.random.fold_in(own, position), (shards_of,), jnp.float32, low / len(shards), top_value / len(shards)))
        factor_of = factor_of * jnp.repeat(steps, dims[position] // shards_of).reshape([-1 if axis == position else 1 for axis in range(len(dims))])
    return factor_of


def scatter_about(stream_key, dims, scale, reach, shards=(), held_as=jnp.bfloat16):
    result = scale * jax.random.normal(stream_key, dims, jnp.float32)
    if shards:
        result = result * steps_of(stream_key, dims, shards, -0.22, 0.18)
    return jnp.clip(result, -reach, reach).astype(held_as)


def heavy_noise(key, dims, scale, reach, shards, heavy, kind=jnp.bfloat16):
    array = scale * jax.random.normal(key, dims, jnp.float32)
    if shards:
        array = array * steps_of(key, dims, shards, -0.22, 0.18)
    return jnp.clip(with_spikes(array, jax.random.fold_in(key, 3), *heavy), -reach, reach).astype(kind)


def setup_inputs(seed: int = 0) -> dict:
    key_list = jax.random.split(jax.random.key(seed), 6)
    return {
        "inputs": draw_inputs(jax.random.fold_in(key_list[5], 71), 0),
        "out_grad": scatter_about(key_list[1], (TOKENS, D_OUT), 1.0, 6.0, ((0, 256),)),
        "w_frozen": scatter_about(key_list[2], (D_IN, D_OUT), D_OUT ** -0.5, 0.09375, ((0, 2),)),
        "adapter_down": heavy_noise(key_list[3], (D_IN, RANK), D_IN ** -0.5, 0.125, ((0, 2),), (0, 1, 2, 2.0)),
        "adapter_up": scatter_about(key_list[4], (RANK, D_OUT), D_OUT ** -0.5, 0.09375, ((0, 2),)),
    }


def reference(inputs, out_grad, w_frozen, adapter_down, adapter_up):
    frozen_part = jnp.dot(out_grad, w_frozen.T, preferred_element_type=jnp.float32)
    latent_grad = jnp.dot(out_grad, adapter_up.T, preferred_element_type=jnp.float32).astype(jnp.bfloat16)
    latent = jnp.dot(inputs, adapter_down, preferred_element_type=jnp.float32).astype(jnp.bfloat16)
    input_grad = (frozen_part + jnp.dot(latent_grad, adapter_down.T, preferred_element_type=jnp.float32)).astype(jnp.bfloat16)
    down_sum = jnp.dot(inputs.T, latent_grad, preferred_element_type=jnp.float32)
    up_sum = jnp.dot(latent.T, out_grad, preferred_element_type=jnp.float32)
    mean_square = (jnp.sum(down_sum * down_sum) + jnp.sum(up_sum * up_sum)) / jnp.float32(D_IN * RANK + RANK * D_OUT)
    clip = jnp.minimum(jnp.float32(1.0), 1.0 / jnp.sqrt(mean_square + 1e-06))
    return (input_grad, (clip * down_sum).astype(jnp.bfloat16), (clip * up_sum).astype(jnp.bfloat16))
```

```python
import jax
import jax.numpy as jnp
from jax import lax
from jax.experimental import pallas as pl
from jax.experimental.pallas import tpu as pltpu
from jax.sharding import PartitionSpec as P

D_IN = 4096
D_OUT = 4096
RANK = 1024
NX, NY, NZ = 4, 4, 8

PARTS = ((0, 384), (384, 384), (768, 256))
ORDERS = (("x1", "y1", "z1"), ("y1", "z1", "x1"), ("z1", "x1", "y1"))
TAIL = ("x2", "y2", "z2", "z4")


def ring_bits(x, y, z, c):
    xs, ys, zs = (x - c) % NX, (y - c) % NY, (z - c) % NZ
    return {
        "x1": ((xs + 1) // 2) % 2,
        "x2": xs // 2,
        "y1": ((ys + 1) // 2) % 2,
        "y2": ys // 2,
        "z1": zs % 2,
        "z2": (zs // 2) % 2,
        "z4": zs // 4,
    }


def partner_pairs(dim):
    pairs = []
    for z in range(NZ):
        for y in range(NY):
            for x in range(NX):
                for c in range(2):
                    x2, y2, z2 = x, y, z
                    if dim[0] == "x":
                        xs = (x - c) % NX
                        ps = xs ^ 1 if dim == "x1" else 3 - xs
                        x2 = (ps + c) % NX
                    elif dim[0] == "y":
                        ys = (y - c) % NY
                        ps = ys ^ 1 if dim == "y1" else 3 - ys
                        y2 = (ps + c) % NY
                    elif dim[0] == "z":
                        zs = (z - c) % NZ
                        z2 = ((zs ^ int(dim[1])) + c) % NZ
                    source = ((z * NY + y) * NX + x) * 2 + c
                    target = ((z2 * NY + y2) * NX + x2) * 2 + c
                    pairs.append((source, target))
    return pairs


PAIRS = {dim: partner_pairs(dim) for dim in ("x1", "x2", "y1", "y2", "z1", "z2", "z4")}


def both_pairs(first, second):
    along = dict(PAIRS[second])
    return [(source, along[target]) for source, target in PAIRS[first]]


def swap(value, dim):
    if dim == "t":
        return lax.ppermute(value, "tensor", [(0, 1), (1, 0)])
    if isinstance(dim, tuple):
        return lax.ppermute(value, ("dp", "tensor"), both_pairs(*dim))
    return lax.ppermute(value, ("dp", "tensor"), PAIRS[dim])


def grads_kernel(where_ref, in_ref, lg_ref, lat_ref, og_ref, *refs):
    out_ref = refs[-1]
    width = out_ref.shape[1]

    def store(rows, product):
        if len(refs) > 1:
            product = product + refs[0][rows].astype(jnp.float32)
        out_ref[rows] = product.astype(out_ref.dtype)

    @pl.when(where_ref[1] == 0)
    def _():
        for k in range(4):
            rows = pl.ds(256 * k, 256)
            store(rows, jnp.dot(in_ref[rows], lg_ref[...], preferred_element_type=jnp.float32))

    @pl.when(where_ref[1] == 1)
    def _():
        for k in range(4):
            store(
                pl.ds(256 * k, 256),
                jnp.dot(lat_ref[...], og_ref[:, k * width : (k + 1) * width], preferred_element_type=jnp.float32),
            )


def quarter_grads(half, kind, operands, part, dtype, recv=None):
    first, width = PARTS[part]
    block = first // width
    in_specs = [
        pl.BlockSpec((1024, 256), lambda j, w: (w[0], 0)),
        pl.BlockSpec((256, width), lambda j, w: (0, block)),
        pl.BlockSpec((256, 256), lambda j, w: (w[0], 0)),
        pl.BlockSpec((256, 4 * width), lambda j, w: (0, block)),
    ]
    if recv is not None:
        in_specs.append(pl.BlockSpec((1024, width), lambda j, w: (0, 0)))
        operands = operands + (recv,)
    return pl.pallas_call(
        grads_kernel,
        out_shape=jax.ShapeDtypeStruct((1024, width), dtype),
        grid_spec=pltpu.PrefetchScalarGridSpec(
            num_scalar_prefetch=1,
            grid=(1,),
            in_specs=in_specs,
            out_specs=pl.BlockSpec((1024, width), lambda j, w: (0, 0)),
        ),
        compiler_params=pltpu.CompilerParams(vmem_limit_bytes=24 * 2**20),
        cost_estimate=pl.CostEstimate(
            flops=2 * 1024 * 256 * width,
            bytes_accessed=1024 * width * jnp.dtype(dtype).itemsize + 2 * 256 * (1024 + 256 + 5 * width),
            transcendentals=0,
        ),
    )(jnp.stack([half, kind]).astype(jnp.int32), *operands)


def place_kernel(where_ref, clip_ref, same_ref, flip_ref, *refs):
    down_ref, up_ref = refs[-2:]
    clip = clip_ref[0]
    width = down_ref.shape[-1]

    def scaled(values):
        return (values.astype(jnp.float32) * clip).astype(jnp.bfloat16)

    def write(for_down, for_up):
        down_ref[0] = scaled(for_down[...])
        for k in range(4):
            up_ref[0, :, k * width : (k + 1) * width] = scaled(for_up[k])

    @pl.when(where_ref[1] == 0)
    def _():
        write(same_ref, flip_ref)

    @pl.when(where_ref[1] == 1)
    def _():
        write(flip_ref, same_ref)


def place(half, kind, clip, part, same, flip, outs):
    first, width = PARTS[part]
    block = first // width
    rows = 64
    quarter = pl.BlockSpec((4, rows, width), lambda g, w, c: (0, g, 0))
    in_specs = [quarter, quarter]
    aliases = {}
    if outs is not None:
        in_specs += [pl.BlockSpec(memory_space=pl.ANY)] * 2
        aliases = {4: 0, 5: 1}
    return pl.pallas_call(
        place_kernel,
        out_shape=(
            jax.ShapeDtypeStruct((2, 4, 256, RANK), jnp.bfloat16),
            jax.ShapeDtypeStruct((2, 256, D_OUT), jnp.bfloat16),
        ),
        grid_spec=pltpu.PrefetchScalarGridSpec(
            num_scalar_prefetch=2,
            grid=(256 // rows,),
            in_specs=in_specs,
            out_specs=(
                pl.BlockSpec((1, 4, rows, width), lambda g, w, c: (w[0], 0, g, block)),
                pl.BlockSpec((1, rows, 4 * width), lambda g, w, c: (w[0], g, block)),
            ),
        ),
        input_output_aliases=aliases,
        cost_estimate=pl.CostEstimate(flops=2**12 * width, bytes_accessed=2**13 * width, transcendentals=0),
    )(
        jnp.stack([half, kind]).astype(jnp.int32),
        clip,
        same.reshape(4, 256, width),
        flip.reshape(4, 256, width),
        *(outs or ()),
    )


def halve(keep, recv, bit):
    rows = keep.shape[0] // 2

    def half(which):
        start = which * rows
        return lax.dynamic_slice_in_dim(keep, start, rows) + lax.dynamic_slice_in_dim(recv, start, rows).astype(jnp.float32)

    return half(1 - bit).astype(jnp.bfloat16), half(bit)


def scatter_four(values, dims, bits):
    rows = values.shape[0] // 4
    me = 2 * bits[dims[0]] + bits[dims[1]]
    total = lax.dynamic_slice_in_dim(values, me * rows, rows)
    for flip, dim in ((3, dims), (2, dims[0]), (1, dims[1])):
        sent = lax.dynamic_slice_in_dim(values, (me ^ flip) * rows, rows).astype(jnp.bfloat16)
        total = total + swap(sent, dim).astype(jnp.float32)
    return total


def gather_four(block, dims, bits):
    both, first, second = swap(block, dims), swap(block, dims[0]), swap(block, dims[1])
    bit = bits[dims[1]]
    return join(join(block, second, bit), join(first, both, bit), bits[dims[0]])


def join(mine, other, bit):
    return jnp.where(bit == 0, jnp.concatenate([mine, other]), jnp.concatenate([other, mine]))


def fill(mine, other, bit, axis):
    size = mine.shape[axis]
    return lax.dynamic_update_slice_in_dim(jnp.concatenate([mine, mine], axis=axis), other, (1 - bit) * size, axis)


def shards(inputs, out_grad, w_frozen, adapter_down, adapter_up):
    core = lax.axis_index("tensor")
    chip = lax.axis_index("dp")
    bits = ring_bits(chip % NX, (chip // NX) % NY, chip // (NX * NY), core)
    parts = range(3)
    dims = [ORDERS[part] for part in parts]
    b0 = [bits[dims[part][0]] for part in parts]
    b1 = [bits[dims[part][1]] for part in parts]
    b2 = [bits[dims[part][2]] for part in parts]

    out_other = swap(out_grad, "t")
    part_latent = jnp.einsum("dr,td->rt", adapter_down, inputs, preferred_element_type=jnp.float32)
    sent = lax.dynamic_slice_in_dim(part_latent, (1 - core) * 512, 512)
    latent_t = (lax.dynamic_slice_in_dim(part_latent, core * 512, 512) + swap(sent, "t")).astype(jnp.bfloat16)
    piece = fill(out_grad, out_other, core, 0)
    grad_half = jnp.einsum("to,ro->tr", piece, adapter_up, preferred_element_type=jnp.float32).astype(jnp.bfloat16)
    latent_grad = fill(grad_half, swap(grad_half, "t"), core, 1)
    operands = (inputs.T, latent_grad, latent_t, piece)

    ahead = [
        swap(quarter_grads(1 - b0[part], 1 - b1[part], operands, part, jnp.bfloat16), dims[part][0]) for part in parts
    ]
    behind = [
        swap(quarter_grads(1 - b0[part], b1[part], operands, part, jnp.bfloat16), dims[part][0]) for part in parts
    ]
    recvs = [
        swap(quarter_grads(b0[part], 1 - b1[part], operands, part, jnp.bfloat16, ahead[part]), dims[part][1])
        for part in parts
    ]
    keeps = [quarter_grads(b0[part], b1[part], operands, part, jnp.float32, behind[part]) for part in parts]
    for part in parts:
        send, keeps[part] = halve(keeps[part], recvs[part], b2[part])
        recvs[part] = swap(send, dims[part][2])
    total = jnp.concatenate(keeps, axis=1) + jnp.concatenate(recvs, axis=1).astype(jnp.float32)
    total = scatter_four(total, ("x2", "y2"), bits)
    block = scatter_four(total, ("z2", "z4"), bits).astype(jnp.bfloat16)

    block = gather_four(block, ("z2", "z4"), bits)
    block = gather_four(block, ("x2", "y2"), bits)
    wide = block.astype(jnp.float32)
    squares = jnp.full((8, 128), jnp.sum(wide * wide))
    for dim in ("x1", "y1", "z1", "t"):
        squares = squares + swap(squares, dim)
    entries = jnp.float32(D_IN * RANK + RANK * D_OUT)
    clip = jnp.minimum(jnp.float32(1.0), 1.0 / jnp.sqrt(squares[0, :1] / entries + 1e-06))
    mine = [block[:, first : first + width] for first, width in PARTS]
    mine = [fill(mine[part], swap(mine[part], dims[part][2]), b2[part], 0) for part in parts]
    second = [swap(mine[part], dims[part][1]) for part in parts]
    third = [swap(mine[part], dims[part][0]) for part in parts]
    fourth = [swap(second[part], dims[part][0]) for part in parts]
    outs = None
    for part in parts:
        outs = place(b0[part], b1[part], clip, part, mine[part], second[part], outs)
    for part in parts:
        outs = place(1 - b0[part], b1[part], clip, part, third[part], fourth[part], outs)

    input_grad = (
        jnp.einsum("to,io->ti", piece, w_frozen, preferred_element_type=jnp.float32)
        + jnp.einsum("tr,dr->td", latent_grad, adapter_down, preferred_element_type=jnp.float32)
    ).astype(jnp.bfloat16)
    return (input_grad, outs[0].reshape(2048, RANK), outs[1].reshape(512, D_OUT))


def solution(mesh):
    in_specs = (
        P("dp", "tensor"),
        P(("dp", "tensor"), None),
        P("tensor", None),
        P("tensor", None),
        P("tensor", None),
    )
    out_specs = (P("dp", "tensor"), P("tensor", None), P("tensor", None))
    return jax.shard_map(shards, mesh=mesh, in_specs=in_specs, out_specs=out_specs, check_vma=False)
```

```python
import functools

import jax
import jax.numpy as jnp
from jax import lax
from jax.experimental import pallas as pl
from jax.experimental.pallas import tpu as pltpu
from jax.sharding import PartitionSpec as P

D_IN = 4096
D_OUT = 4096
RANK = 1024
NX, NY, NZ = 4, 4, 8

PARTS = ((0, 384), (384, 384), (768, 256))
ORDERS = (("x1", "y1", "z1"), ("y1", "z1", "x1"), ("z1", "x1", "y1"))
TAIL = ("x2", "y2", "z2", "z4")


def ring_bits(chip, core):
    xs = ((chip & (NX - 1)) - core) & (NX - 1)
    ys = (((chip >> 2) & (NY - 1)) - core) & (NY - 1)
    zs = ((chip >> 4) - core) & (NZ - 1)
    return {
        "x1": ((xs + 1) >> 1) & 1,
        "x2": xs >> 1,
        "y1": ((ys + 1) >> 1) & 1,
        "y2": ys >> 1,
        "z1": zs & 1,
        "z2": (zs >> 1) & 1,
        "z4": zs >> 2,
    }


def partner_pairs(dim):
    pairs = []
    for z in range(NZ):
        for y in range(NY):
            for x in range(NX):
                for c in range(2):
                    x2, y2, z2 = x, y, z
                    if dim[0] == "x":
                        xs = (x - c) % NX
                        ps = xs ^ 1 if dim == "x1" else 3 - xs
                        x2 = (ps + c) % NX
                    elif dim[0] == "y":
                        ys = (y - c) % NY
                        ps = ys ^ 1 if dim == "y1" else 3 - ys
                        y2 = (ps + c) % NY
                    elif dim[0] == "z":
                        zs = (z - c) % NZ
                        z2 = ((zs ^ int(dim[1])) + c) % NZ
                    source = ((z * NY + y) * NX + x) * 2 + c
                    target = ((z2 * NY + y2) * NX + x2) * 2 + c
                    pairs.append((source, target))
    return pairs


PAIRS = {dim: partner_pairs(dim) for dim in ("x1", "x2", "y1", "y2", "z1", "z2", "z4")}


def both_pairs(first, second):
    along = dict(PAIRS[second])
    return [(source, along[target]) for source, target in PAIRS[first]]


def swap(value, dim):
    if dim == "t":
        return lax.ppermute(value, "tensor", [(0, 1), (1, 0)])
    if isinstance(dim, tuple):
        return lax.ppermute(value, ("dp", "tensor"), both_pairs(*dim))
    return lax.ppermute(value, ("dp", "tensor"), PAIRS[dim])


def grads_kernel(part, flip_kind, spots_ref, in_ref, lg_ref, lat_ref, og_ref, *refs):
    out_ref = refs[-1]
    width = out_ref.shape[1]
    kind = spots_ref[3 + part] ^ flip_kind

    def store(rows, product):
        if len(refs) > 1:
            product = product + refs[0][rows].astype(jnp.float32)
        out_ref[rows] = product.astype(out_ref.dtype)

    @pl.when(kind == 0)
    def _():
        for k in range(4):
            rows = pl.ds(256 * k, 256)
            store(rows, jnp.dot(in_ref[rows], lg_ref[...], preferred_element_type=jnp.float32))

    @pl.when(kind == 1)
    def _():
        for k in range(4):
            store(
                pl.ds(256 * k, 256),
                jnp.dot(lat_ref[...], og_ref[:, k * width : (k + 1) * width], preferred_element_type=jnp.float32),
            )


def quarter_grads(spots, flip_half, flip_kind, operands, part, dtype, recv=None):
    first, width = PARTS[part]
    block = first // width
    in_specs = [
        pl.BlockSpec((1024, 256), lambda j, s: (s[part] ^ flip_half, 0)),
        pl.BlockSpec((256, width), lambda j, s: (0, block)),
        pl.BlockSpec((256, 256), lambda j, s: (s[part] ^ flip_half, 0)),
        pl.BlockSpec((256, 4 * width), lambda j, s: (0, block)),
    ]
    if recv is not None:
        in_specs.append(pl.BlockSpec((1024, width), lambda j, s: (0, 0)))
        operands = operands + (recv,)
    return pl.pallas_call(
        functools.partial(grads_kernel, part, flip_kind),
        out_shape=jax.ShapeDtypeStruct((1024, width), dtype),
        grid_spec=pltpu.PrefetchScalarGridSpec(
            num_scalar_prefetch=1,
            grid=(1,),
            in_specs=in_specs,
            out_specs=pl.BlockSpec((1024, width), lambda j, s: (0, 0)),
        ),
        compiler_params=pltpu.CompilerParams(vmem_limit_bytes=24 * 2**20),
        cost_estimate=pl.CostEstimate(
            flops=2 * 1024 * 256 * width,
            bytes_accessed=1024 * width * jnp.dtype(dtype).itemsize + 2 * 256 * (1024 + 256 + 5 * width),
            transcendentals=0,
        ),
    )(spots, *operands)


def place_kernel(entries, spots_ref, clip_ref, *refs):
    count = len(entries)
    ins, (down_ref, up_ref), buffers = refs[:count], refs[-count - 4 : -count - 2], refs[-count - 2 : -2]
    in_sems, out_sems = refs[-2:]
    clip = clip_ref[0]
    loads = [pltpu.make_async_copy(ins[n], buffers[n], in_sems.at[n]) for n in range(count)]
    for load in loads:
        load.start()

    def stores(n, kind):
        part, flip_half, _ = entries[n]
        first, width = PARTS[part]
        half = spots_ref[part] ^ flip_half
        copies = []
        for k in range(4):
            start = 4 * first + k * width
            if kind == 0:
                target = down_ref.at[half, k, :, pl.ds(first, width)]
            else:
                target = up_ref.at[half, :, pl.ds(start, width)]
            copies.append(pltpu.make_async_copy(buffers[n].at[k], target, out_sems.at[n, k]))
        return copies

    def each(n, act):
        own_kind = spots_ref[3 + entries[n][0]] ^ entries[n][2]
        for kind in range(2):

            @pl.when(own_kind == kind)
            def _(kind=kind):
                for copy in stores(n, kind):
                    act(copy)

    for n in range(count):
        loads[n].wait()
        for k in range(4):
            buffers[n][k] = (buffers[n][k].astype(jnp.float32) * clip).astype(jnp.bfloat16)
        each(n, lambda copy: copy.start())
    for n in range(count):
        each(n, lambda copy: copy.wait())


def place(spots, clip, entries, outs):
    values = [entry[3].reshape(4, 256, PARTS[entry[0]][1]) for entry in entries]
    anywhere = pl.BlockSpec(memory_space=pl.ANY)
    aliases = {}
    if outs is not None:
        aliases = {2 + len(entries): 0, 3 + len(entries): 1}
        values += outs
    smem = pl.BlockSpec(memory_space=pltpu.SMEM)
    size = sum(1024 * PARTS[entry[0]][1] for entry in entries)
    return pl.pallas_call(
        functools.partial(place_kernel, [entry[:3] for entry in entries]),
        out_shape=(
            jax.ShapeDtypeStruct((2, 4, 256, RANK), jnp.bfloat16),
            jax.ShapeDtypeStruct((2, 256, D_OUT), jnp.bfloat16),
        ),
        in_specs=[smem, smem] + [anywhere] * len(values),
        out_specs=(anywhere, anywhere),
        scratch_shapes=[pltpu.VMEM((4, 256, PARTS[entry[0]][1]), jnp.bfloat16) for entry in entries]
        + [pltpu.SemaphoreType.DMA((len(entries),)), pltpu.SemaphoreType.DMA((len(entries), 4))],
        input_output_aliases=aliases,
        compiler_params=pltpu.CompilerParams(vmem_limit_bytes=24 * 2**20),
        cost_estimate=pl.CostEstimate(flops=size, bytes_accessed=4 * size, transcendentals=0),
    )(spots, clip, *values)


def halve(keep, recv, bit):
    rows = keep.shape[0] // 2

    def half(which):
        start = which * rows
        return lax.dynamic_slice_in_dim(keep, start, rows) + lax.dynamic_slice_in_dim(recv, start, rows).astype(jnp.float32)

    return half(1 - bit).astype(jnp.bfloat16), half(bit)


def scatter_four(values, dims, bits, beside):
    rows = values.shape[0] // 4
    me = 2 * bits[dims[0]] + bits[dims[1]]
    flips = ((3, dims), (2, dims[0]), (1, dims[1]))
    sends = [lax.dynamic_slice_in_dim(values, (me ^ flip) * rows, rows).astype(jnp.bfloat16) for flip, _ in flips]
    recvs = beside(sends, lambda sends: [swap(sent, dim) for sent, (_, dim) in zip(sends, flips)])
    total = lax.dynamic_slice_in_dim(values, me * rows, rows)
    return total + sum(recv.astype(jnp.float32) for recv in recvs)


def gather_four(block, dims, bits, beside):
    both, first, second = beside(block, lambda block: [swap(block, dim) for dim in (dims, *dims)])
    bit = bits[dims[1]]
    return join(join(block, second, bit), join(first, both, bit), bits[dims[0]])


def join(mine, other, bit):
    return jnp.where(bit == 0, jnp.concatenate([mine, other]), jnp.concatenate([other, mine]))


def fill(mine, other, bit, axis):
    size = mine.shape[axis]
    return lax.dynamic_update_slice_in_dim(jnp.concatenate([mine, mine], axis=axis), other, (1 - bit) * size, axis)


def shards(inputs, out_grad, w_frozen, adapter_down, adapter_up):
    core = lax.axis_index("tensor")
    chip = lax.axis_index("dp")
    bits = ring_bits(chip, core)
    parts = range(3)
    dims = [ORDERS[part] for part in parts]
    b0 = [bits[dims[part][0]] for part in parts]
    b1 = [bits[dims[part][1]] for part in parts]
    b2 = [bits[dims[part][2]] for part in parts]

    out_other = swap(out_grad, "t")
    part_latent = jnp.einsum("dr,td->rt", adapter_down, inputs, preferred_element_type=jnp.float32)
    sent = lax.dynamic_slice_in_dim(part_latent, (1 - core) * 512, 512)
    latent_t = (lax.dynamic_slice_in_dim(part_latent, core * 512, 512) + swap(sent, "t")).astype(jnp.bfloat16)
    piece = fill(out_grad, out_other, core, 0)
    grad_half = jnp.einsum("to,ro->tr", piece, adapter_up, preferred_element_type=jnp.float32).astype(jnp.bfloat16)
    latent_grad = fill(grad_half, swap(grad_half, "t"), core, 1)
    operands = (inputs.T, latent_grad, latent_t, piece)
    spots = jnp.stack(b0 + b1).astype(jnp.int32)

    grads = []

    def beside(values, exchange):
        rows = slice(len(grads) * 512, len(grads) * 512 + 512)
        values, piece_now, latent_now = lax.optimization_barrier((values, piece, latent_grad))
        part_grad = (
            jnp.einsum("to,io->ti", piece_now, w_frozen[rows], preferred_element_type=jnp.float32)
            + jnp.einsum("tr,dr->td", latent_now, adapter_down[rows], preferred_element_type=jnp.float32)
        ).astype(jnp.bfloat16)
        values, part_grad = lax.optimization_barrier((exchange(values), part_grad))
        grads.append(part_grad)
        return values

    ahead = [swap(quarter_grads(spots, 1, 1, operands, part, jnp.bfloat16), dims[part][0]) for part in parts]
    behind = [swap(quarter_grads(spots, 1, 0, operands, part, jnp.bfloat16), dims[part][0]) for part in parts]
    recvs = [
        swap(quarter_grads(spots, 0, 1, operands, part, jnp.bfloat16, ahead[part]), dims[part][1]) for part in parts
    ]
    keeps = [quarter_grads(spots, 0, 0, operands, part, jnp.float32, behind[part]) for part in parts]
    for part in parts:
        send, keeps[part] = halve(keeps[part], recvs[part], b2[part])
        recvs[part] = swap(send, dims[part][2])
    total = jnp.concatenate(keeps, axis=1) + jnp.concatenate(recvs, axis=1).astype(jnp.float32)
    total = scatter_four(total, ("x2", "y2"), bits, beside)
    block = scatter_four(total, ("z2", "z4"), bits, beside).astype(jnp.bfloat16)

    block = gather_four(block, ("z2", "z4"), bits, beside)
    block = gather_four(block, ("x2", "y2"), bits, beside)
    mine = [block[:, first : first + width] for first, width in PARTS]
    arrived = [swap(mine[part], dims[part][2]) for part in parts]
    wide = block.astype(jnp.float32)
    squares = jnp.full((8, 128), jnp.sum(wide * wide))
    squares = squares + swap(squares, "x1")
    arrived, squares = lax.optimization_barrier((arrived, squares))
    mine = [fill(mine[part], arrived[part], b2[part], 0) for part in parts]
    second = [swap(mine[part], dims[part][1]) for part in parts]
    mine, squares = lax.optimization_barrier((mine, squares))
    third = [swap(mine[part], dims[part][0]) for part in parts]
    squares = squares + swap(squares, "y1")
    second, squares = lax.optimization_barrier((second, squares))
    fourth = [swap(second[part], dims[part][0]) for part in parts]
    for dim in ("z1", "t"):
        squares = squares + swap(squares, dim)
    entries = jnp.float32(D_IN * RANK + RANK * D_OUT)
    clip = jnp.minimum(jnp.float32(1.0), 1.0 / jnp.sqrt(squares[0, :1] / entries + 1e-06))
    outs = place(spots, clip, [e for part in parts for e in ((part, 0, 0, mine[part]), (part, 0, 1, second[part]))], None)
    outs = place(spots, clip, [(part, 1, 0, third[part]) for part in parts], outs)
    outs = place(spots, clip, [(part, 1, 1, fourth[part]) for part in parts], outs)

    input_grad = jnp.concatenate(grads, axis=1)
    return (input_grad, outs[0].reshape(2048, RANK), outs[1].reshape(512, D_OUT))


def solution(mesh):
    in_specs = (
        P("dp", "tensor"),
        P(("dp", "tensor"), None),
        P("tensor", None),
        P("tensor", None),
        P("tensor", None),
    )
    out_specs = (P("dp", "tensor"), P("tensor", None), P("tensor", None))
    return jax.shard_map(shards, mesh=mesh, in_specs=in_specs, out_specs=out_specs, check_vma=False)
```

```python
import functools

import jax
import jax.numpy as jnp
from jax import lax
from jax.experimental import pallas as pl
from jax.experimental.pallas import tpu as pltpu
from jax.sharding import PartitionSpec as P

D_IN = 4096
D_OUT = 4096
RANK = 1024
NX, NY, NZ = 4, 4, 8

PARTS = ((0, 384), (384, 384), (768, 256))
ORDERS = (("x1", "y1", "z1"), ("y1", "z1", "x1"), ("z1", "x1", "y1"))
TAIL = ("x2", "y2", "z2", "z4")


def ring_bits(chip, core):
    xs = ((chip & (NX - 1)) - core) & (NX - 1)
    ys = (((chip >> 2) & (NY - 1)) - core) & (NY - 1)
    zs = ((chip >> 4) - core) & (NZ - 1)
    return {
        "x1": ((xs + 1) >> 1) & 1,
        "x2": xs >> 1,
        "y1": ((ys + 1) >> 1) & 1,
        "y2": ys >> 1,
        "z1": zs & 1,
        "z2": (zs >> 1) & 1,
        "z4": zs >> 2,
    }


def partner_pairs(dim):
    pairs = []
    for z in range(NZ):
        for y in range(NY):
            for x in range(NX):
                for c in range(2):
                    x2, y2, z2 = x, y, z
                    if dim[0] == "x":
                        xs = (x - c) % NX
                        ps = xs ^ 1 if dim == "x1" else 3 - xs
                        x2 = (ps + c) % NX
                    elif dim[0] == "y":
                        ys = (y - c) % NY
                        ps = ys ^ 1 if dim == "y1" else 3 - ys
                        y2 = (ps + c) % NY
                    elif dim[0] == "z":
                        zs = (z - c) % NZ
                        z2 = ((zs ^ int(dim[1])) + c) % NZ
                    source = ((z * NY + y) * NX + x) * 2 + c
                    target = ((z2 * NY + y2) * NX + x2) * 2 + c
                    pairs.append((source, target))
    return pairs


PAIRS = {dim: partner_pairs(dim) for dim in ("x1", "x2", "y1", "y2", "z1", "z2", "z4")}


def both_pairs(first, second):
    along = dict(PAIRS[second])
    return [(source, along[target]) for source, target in PAIRS[first]]


def swap(value, dim):
    if dim == "t":
        return lax.ppermute(value, "tensor", [(0, 1), (1, 0)])
    if isinstance(dim, tuple):
        return lax.ppermute(value, ("dp", "tensor"), both_pairs(*dim))
    return lax.ppermute(value, ("dp", "tensor"), PAIRS[dim])


def grads_kernel(part, stage, spots_ref, in_ref, lg_ref, lat_ref, og_ref, *refs):
    width = PARTS[part][1]

    def down(k):
        rows = pl.ds(256 * k, 256)
        return jnp.dot(in_ref[rows], lg_ref[...], preferred_element_type=jnp.float32)

    def up(k):
        return jnp.dot(lat_ref[...], og_ref[:, k * width : (k + 1) * width], preferred_element_type=jnp.float32)

    if stage == "first":
        (first_ref,) = refs
        for k in range(4):
            first_ref[0, k] = down(k).astype(jnp.bfloat16)
            first_ref[1, k] = up(k).astype(jnp.bfloat16)
        return

    def run(product):
        for k in range(2 if stage in ("third", "own") else 4):
            total = product(k)
            if stage in ("ahead", "behind"):
                refs[0][k] = total.astype(jnp.bfloat16)
                continue
            total = total + refs[0][0, k].astype(jnp.float32)
            if stage == "second":
                refs[1][k] = total.astype(jnp.bfloat16)
                continue
            refs[2][k] = (total + refs[1][k].astype(jnp.float32)).astype(refs[2].dtype)

    kind = spots_ref[3 + part] ^ (stage in ("ahead", "second"))
    pl.when(kind == 0)(functools.partial(run, down))
    pl.when(kind == 1)(functools.partial(run, up))


def grads(spots, operands, part, stage, *recvs):
    first, width = PARTS[part]
    block = first // width
    other_half = int(stage in ("first", "ahead", "behind"))
    other_kind = int(stage in ("ahead", "second"))
    count = 2 if stage in ("third", "own") else 4

    def piece_of(s):
        return s[6 + part] ^ int(stage == "third") if count == 2 else 0

    pieces = 4 // count
    in_specs = [
        pl.BlockSpec((256 * count, 256), lambda j, s: ((s[part] ^ other_half) * pieces + piece_of(s), 0)),
        pl.BlockSpec((256, width), lambda j, s: (0, block)),
        pl.BlockSpec((256, 256), lambda j, s: (s[part] ^ other_half, 0)),
        pl.BlockSpec((256, count * width), lambda j, s: (0, block * pieces + piece_of(s))),
    ]
    recvs = list(recvs)
    if recvs:
        both = recvs[0].ndim == 4
        recvs[0] = recvs[0].reshape(-1, 4, 256, width)
        in_specs.append(
            pl.BlockSpec(
                (1, count, 256, width), lambda j, s: (s[3 + part] ^ other_kind if both else 0, piece_of(s), 0, 0)
            )
        )
    if count == 2:
        in_specs.append(pl.BlockSpec((2, 256, width), lambda j, s: (piece_of(s), 0, 0)))
    shape = (2, 4, 256, width) if stage == "first" else (count, 256, width)
    dtype = jnp.float32 if stage == "own" else jnp.bfloat16
    products = len(shape) - 2 if stage == "first" else count / 4
    return pl.pallas_call(
        functools.partial(grads_kernel, part, stage),
        out_shape=jax.ShapeDtypeStruct(shape, dtype),
        grid_spec=pltpu.PrefetchScalarGridSpec(
            num_scalar_prefetch=1,
            grid=(1,),
            in_specs=in_specs,
            out_specs=pl.BlockSpec(shape, lambda j, s: (0,) * len(shape)),
        ),
        compiler_params=pltpu.CompilerParams(vmem_limit_bytes=10 * 2**20),
        cost_estimate=pl.CostEstimate(
            flops=int(2 * 1024 * 256 * width * products),
            bytes_accessed=int(2048 * width * products) + 2 * 256 * (1024 + 256 + 5 * width),
            transcendentals=0,
        ),
    )(spots, *operands, *recvs)


def squares_kernel(*refs):
    total = jnp.zeros((8, 128), jnp.float32)
    for ref in refs[:-1]:
        rows, width = ref.shape
        for column in range(0, width, 128):

            def add(step, total, ref=ref, column=column):
                values = ref[pl.ds(pl.multiple_of(step * 128, 128), 128), column : column + 128].astype(jnp.float32)
                return total + jnp.sum((values * values).reshape(16, 8, 128), axis=0)

            total = lax.fori_loop(0, rows // 128, add, total)
    refs[-1][...] = total


def squares_of(values):
    size = sum(value.size for value in values)
    return pl.pallas_call(
        squares_kernel,
        out_shape=jax.ShapeDtypeStruct((8, 128), jnp.float32),
        grid=(1,),
        in_specs=[pl.BlockSpec(value.shape, lambda j: (0, 0)) for value in values],
        out_specs=pl.BlockSpec((8, 128), lambda j: (0, 0)),
        compiler_params=pltpu.CompilerParams(vmem_limit_bytes=12 * 2**20),
        cost_estimate=pl.CostEstimate(flops=2 * size, bytes_accessed=2 * size, transcendentals=0),
    )(*values)


def place_kernel(entries, spots_ref, squares_ref, *refs):
    count = len(entries)
    ins, (down_ref, up_ref), buffers = refs[:count], refs[count : count + 2], refs[count + 2 : -1]
    out_sems = refs[-1]

    def stores(n, kind):
        part, flip_half, _ = entries[n]
        first, width = PARTS[part]
        half = spots_ref[part] ^ flip_half
        copies = []
        for k in range(4):
            start = 4 * first + k * width
            if kind == 0:
                target = down_ref.at[half, k, :, pl.ds(first, width)]
            else:
                target = up_ref.at[half, :, pl.ds(start, width)]
            copies.append(pltpu.make_async_copy(buffers[n].at[k], target, out_sems.at[n, k]))
        return copies

    def each(n, act):
        own_kind = spots_ref[3 + entries[n][0]] ^ entries[n][2]
        for kind in range(2):

            @pl.when(own_kind == kind)
            def _(kind=kind):
                for copy in stores(n, kind):
                    act(copy)

    entries_in_all = jnp.float32(D_IN * RANK + RANK * D_OUT)
    mean_square = jnp.sum(squares_ref[...], keepdims=True) / entries_in_all
    clip = jnp.minimum(jnp.float32(1.0), 1.0 / jnp.sqrt(mean_square + 1e-06))
    for n in range(count):
        for k in range(4):
            buffers[n][k] = (ins[n][k].astype(jnp.float32) * clip).astype(jnp.bfloat16)
        each(n, lambda copy: copy.start())
    for n in range(count):
        each(n, lambda copy: copy.wait())


def place(spots, squares, entries):
    values = [entry[3].reshape(4, 256, PARTS[entry[0]][1]) for entry in entries]
    anywhere = pl.BlockSpec(memory_space=pl.ANY)
    smem = pl.BlockSpec(memory_space=pltpu.SMEM)
    size = sum(1024 * PARTS[entry[0]][1] for entry in entries)
    return pl.pallas_call(
        functools.partial(place_kernel, [entry[:3] for entry in entries]),
        out_shape=(
            jax.ShapeDtypeStruct((2, 4, 256, RANK), jnp.bfloat16),
            jax.ShapeDtypeStruct((2, 256, D_OUT), jnp.bfloat16),
        ),
        in_specs=[smem] + [pl.BlockSpec(memory_space=pltpu.VMEM)] * (1 + len(values)),
        out_specs=(anywhere, anywhere),
        scratch_shapes=[pltpu.VMEM((4, 256, PARTS[entry[0]][1]), jnp.bfloat16) for entry in entries]
        + [pltpu.SemaphoreType.DMA((len(entries), 4))],
        compiler_params=pltpu.CompilerParams(vmem_limit_bytes=20 * 2**20),
        cost_estimate=pl.CostEstimate(flops=size, bytes_accessed=4 * size, transcendentals=0),
    )(spots, squares, *values)


def scatter_four(values, dims, bits, beside):
    rows = values.shape[0] // 4
    me = 2 * bits[dims[0]] + bits[dims[1]]
    own, *sends = [lax.dynamic_slice_in_dim(values, (me ^ flip) * rows, rows) for flip in (0, 3, 2, 1)]
    sends = [send.astype(jnp.bfloat16) for send in sends]
    recvs = beside(sends, lambda sends: [swap(send, dim) for send, dim in zip(sends, (dims, *dims))])
    return own + sum(recv.astype(jnp.float32) for recv in recvs)


def gather_four(block, dims, bits, beside):
    both, first, second = beside(block, lambda block: [swap(block, dim) for dim in (dims, *dims)])
    bit = bits[dims[1]]
    return join(join(block, second, bit), join(first, both, bit), bits[dims[0]])


def join(mine, other, bit):
    return jnp.where(bit == 0, jnp.concatenate([mine, other]), jnp.concatenate([other, mine]))


def fill(mine, other, bit, axis):
    size = mine.shape[axis]
    return lax.dynamic_update_slice_in_dim(jnp.concatenate([mine, mine], axis=axis), other, (1 - bit) * size, axis)


def shards(inputs, out_grad, w_frozen, adapter_down, adapter_up):
    core = lax.axis_index("tensor")
    chip = lax.axis_index("dp")
    bits = ring_bits(chip, core)
    parts = range(3)
    dims = [ORDERS[part] for part in parts]
    b0 = [bits[dims[part][0]] for part in parts]
    b1 = [bits[dims[part][1]] for part in parts]
    b2 = [bits[dims[part][2]] for part in parts]

    out_other = swap(out_grad, "t")
    part_latent = jnp.einsum("dr,td->rt", adapter_down, inputs, preferred_element_type=jnp.float32)
    sent = lax.dynamic_slice_in_dim(part_latent, (1 - core) * 512, 512)
    latent_t = (lax.dynamic_slice_in_dim(part_latent, core * 512, 512) + swap(sent, "t")).astype(jnp.bfloat16)
    piece = join(out_grad, out_other, core)
    grad_half = jnp.einsum("to,ro->tr", piece, adapter_up, preferred_element_type=jnp.float32).astype(jnp.bfloat16)
    latent_grad = fill(grad_half, swap(grad_half, "t"), core, 1)
    operands = (inputs.T, latent_grad, latent_t, piece)
    spots = jnp.stack(b0 + b1 + b2 + [2 * bits["x2"] + bits["y2"]]).astype(jnp.int32)

    pieces = []

    def beside(values, exchange):
        rows = slice(len(pieces) * 512, len(pieces) * 512 + 512)
        values, piece_now, latent_now = lax.optimization_barrier((values, piece, latent_grad))
        part_grad = (
            jnp.einsum("to,io->ti", piece_now, w_frozen[rows], preferred_element_type=jnp.float32)
            + jnp.einsum("tr,dr->td", latent_now, adapter_down[rows], preferred_element_type=jnp.float32)
        ).astype(jnp.bfloat16)
        values, part_grad = lax.optimization_barrier((exchange(values), part_grad))
        pieces.append(part_grad)
        return values

    ahead, behind = [None] * 3, [None] * 3
    for part in (0, 1):
        ahead[part] = swap(grads(spots, operands, part, "ahead"), dims[part][0])
    ahead[2] = behind[2] = swap(grads(spots, operands, 2, "first"), dims[2][0])
    for part in (0, 1):
        ready = grads(spots, operands, part, "behind")
        behind[part] = swap(ready, dims[part][0])
    recvs = []
    for part in parts:
        if part == 2:
            (recv, behind), _ = lax.optimization_barrier(((ahead[part], behind), ready))
        else:
            recv, _ = lax.optimization_barrier((ahead[part], ready))
        ready = grads(spots, operands, part, "second", recv)
        recvs.append(swap(ready, dims[part][1]))
    keeps = [None] * 3
    for part in (1, 0, 2):
        recv, _ = lax.optimization_barrier((recvs[part], ready))
        ready = grads(spots, operands, part, "third", behind[part], recv)
        keeps[part] = behind[part], recv
        recvs[part] = swap(ready, dims[part][2])
    for part in parts:
        kept, _ = lax.optimization_barrier((keeps[part], ready))
        keeps[part] = grads(spots, operands, part, "own", *kept)

    def side_by_side(values):
        return jnp.concatenate([value.reshape(512, -1) for value in values], axis=1).astype(jnp.float32)

    own = side_by_side(keeps) + side_by_side(recvs)
    own = scatter_four(own, ("x2", "y2"), bits, beside)
    own = scatter_four(own, ("z2", "z4"), bits, beside)
    block = own.astype(jnp.bfloat16)

    block = gather_four(block, ("z2", "z4"), bits, beside)
    block = gather_four(block, ("x2", "y2"), bits, beside)
    mine = [block[:, first : first + width] for first, width in PARTS]
    mine = [fill(mine[part], swap(mine[part], dims[part][2]), b2[part], 0) for part in parts]
    second = [swap(mine[part], dims[part][1]) for part in parts]
    third = [swap(mine[part], dims[part][0]) for part in (0, 1)]
    fourth = [swap(second[part], dims[part][0]) for part in (0, 1)]
    last = swap(jnp.concatenate([mine[2], second[2]]), dims[2][0])

    squares = squares_of(mine + second) + squares_of(third + [last]) + squares_of(fourth)
    squares = squares + swap(squares, "t")
    third.append(last[:1024])
    fourth.append(last[1024:])
    quarters = [
        (part, flip_half, flip_kind, values[part])
        for flip_half, flip_kind, values in ((0, 0, mine), (0, 1, second), (1, 0, third), (1, 1, fourth))
        for part in parts
    ]
    outs = place(spots, squares, quarters)

    input_grad = jnp.concatenate(pieces, axis=1)
    return (input_grad, outs[0].reshape(2048, RANK), outs[1].reshape(512, D_OUT))


def solution(mesh):
    in_specs = (
        P("dp", "tensor"),
        P(("dp", "tensor"), None),
        P("tensor", None),
        P("tensor", None),
        P("tensor", None),
    )
    out_specs = (P("dp", "tensor"), P("tensor", None), P("tensor", None))
    return jax.shard_map(shards, mesh=mesh, in_specs=in_specs, out_specs=out_specs, check_vma=False)
```

```python
import functools

import jax
import jax.numpy as jnp
from jax import lax
from jax.experimental import pallas as pl
from jax.experimental.pallas import tpu as pltpu
from jax.sharding import PartitionSpec as P

D_IN = 4096
D_OUT = 4096
RANK = 1024
NX, NY, NZ = 4, 4, 8

PARTS = ((0, 384), (384, 384), (768, 256))
ORDERS = (("x1", "y1", "z1"), ("y1", "z1", "x1"), ("z1", "x1", "y1"))
TAIL = ("x2", "y2", "z2", "z4")


def ring_bits(chip, core):
    xs = ((chip & (NX - 1)) - core) & (NX - 1)
    ys = (((chip >> 2) & (NY - 1)) - core) & (NY - 1)
    zs = ((chip >> 4) - core) & (NZ - 1)
    return {
        "x1": ((xs + 1) >> 1) & 1,
        "x2": xs >> 1,
        "y1": ((ys + 1) >> 1) & 1,
        "y2": ys >> 1,
        "z1": zs & 1,
        "z2": (zs >> 1) & 1,
        "z4": zs >> 2,
    }


def partner_pairs(dim):
    pairs = []
    for z in range(NZ):
        for y in range(NY):
            for x in range(NX):
                for c in range(2):
                    x2, y2, z2 = x, y, z
                    if dim[0] == "x":
                        xs = (x - c) % NX
                        ps = xs ^ 1 if dim == "x1" else 3 - xs
                        x2 = (ps + c) % NX
                    elif dim[0] == "y":
                        ys = (y - c) % NY
                        ps = ys ^ 1 if dim == "y1" else 3 - ys
                        y2 = (ps + c) % NY
                    elif dim[0] == "z":
                        zs = (z - c) % NZ
                        z2 = ((zs ^ int(dim[1])) + c) % NZ
                    source = ((z * NY + y) * NX + x) * 2 + c
                    target = ((z2 * NY + y2) * NX + x2) * 2 + c
                    pairs.append((source, target))
    return pairs


PAIRS = {dim: partner_pairs(dim) for dim in ("x1", "x2", "y1", "y2", "z1", "z2", "z4")}


def both_pairs(first, second):
    along = dict(PAIRS[second])
    return [(source, along[target]) for source, target in PAIRS[first]]


def swap(value, dim):
    if dim == "t":
        return lax.ppermute(value, "tensor", [(0, 1), (1, 0)])
    if isinstance(dim, tuple):
        return lax.ppermute(value, ("dp", "tensor"), both_pairs(*dim))
    return lax.ppermute(value, ("dp", "tensor"), PAIRS[dim])


def grads_kernel(part, stage, spots_ref, in_ref, lg_ref, lat_ref, og_ref, *refs):
    width = PARTS[part][1]

    def down(k):
        rows = pl.ds(256 * k, 256)
        return jnp.dot(in_ref[rows], lg_ref[...], preferred_element_type=jnp.float32)

    def up(k):
        return jnp.dot(lat_ref[...], og_ref[:, k * width : (k + 1) * width], preferred_element_type=jnp.float32)

    if stage == "first":
        (first_ref,) = refs
        for k in range(4):
            first_ref[0, k] = down(k).astype(jnp.bfloat16)
            first_ref[1, k] = up(k).astype(jnp.bfloat16)
        return

    def run(product):
        for k in range(2 if stage in ("third", "own") else 4):
            total = product(k)
            if stage in ("ahead", "behind"):
                refs[0][k] = total.astype(jnp.bfloat16)
                continue
            total = total + refs[0][0, k].astype(jnp.float32)
            if stage == "second":
                refs[1][k] = total.astype(jnp.bfloat16)
                continue
            refs[2][k] = (total + refs[1][k].astype(jnp.float32)).astype(refs[2].dtype)

    kind = spots_ref[3 + part] ^ (stage in ("ahead", "second"))
    pl.when(kind == 0)(functools.partial(run, down))
    pl.when(kind == 1)(functools.partial(run, up))


def grads(spots, operands, part, stage, *recvs):
    first, width = PARTS[part]
    block = first // width
    other_half = int(stage in ("first", "ahead", "behind"))
    other_kind = int(stage in ("ahead", "second"))
    count = 2 if stage in ("third", "own") else 4

    def piece_of(s):
        return s[6 + part] ^ int(stage == "third") if count == 2 else 0

    pieces = 4 // count
    in_specs = [
        pl.BlockSpec((256 * count, 256), lambda j, s: ((s[part] ^ other_half) * pieces + piece_of(s), 0)),
        pl.BlockSpec((256, width), lambda j, s: (0, block)),
        pl.BlockSpec((256, 256), lambda j, s: (s[part] ^ other_half, 0)),
        pl.BlockSpec((256, count * width), lambda j, s: (0, block * pieces + piece_of(s))),
    ]
    recvs = list(recvs)
    if recvs:
        both = recvs[0].ndim == 4
        recvs[0] = recvs[0].reshape(-1, 4, 256, width)
        in_specs.append(
            pl.BlockSpec(
                (1, count, 256, width), lambda j, s: (s[3 + part] ^ other_kind if both else 0, piece_of(s), 0, 0)
            )
        )
    if count == 2:
        in_specs.append(pl.BlockSpec((2, 256, width), lambda j, s: (piece_of(s), 0, 0)))
    shape = (2, 4, 256, width) if stage == "first" else (count, 256, width)
    dtype = jnp.float32 if stage == "own" else jnp.bfloat16
    products = len(shape) - 2 if stage == "first" else count / 4
    return pl.pallas_call(
        functools.partial(grads_kernel, part, stage),
        out_shape=jax.ShapeDtypeStruct(shape, dtype),
        grid_spec=pltpu.PrefetchScalarGridSpec(
            num_scalar_prefetch=1,
            grid=(1,),
            in_specs=in_specs,
            out_specs=pl.BlockSpec(shape, lambda j, s: (0,) * len(shape)),
        ),
        compiler_params=pltpu.CompilerParams(vmem_limit_bytes=10 * 2**20),
        cost_estimate=pl.CostEstimate(
            flops=int(2 * 1024 * 256 * width * products),
            bytes_accessed=int(2048 * width * products) + 2 * 256 * (1024 + 256 + 5 * width),
            transcendentals=0,
        ),
    )(spots, *operands, *recvs)


def squares_kernel(*refs):
    total = jnp.zeros((8, 128), jnp.float32)
    for ref in refs[:-1]:
        rows, width = ref.shape
        for column in range(0, width, 128):

            def add(step, total, ref=ref, column=column):
                values = ref[pl.ds(pl.multiple_of(step * 128, 128), 128), column : column + 128].astype(jnp.float32)
                return total + jnp.sum((values * values).reshape(16, 8, 128), axis=0)

            total = lax.fori_loop(0, rows // 128, add, total)
    refs[-1][...] = total


def squares_of(values):
    size = sum(value.size for value in values)
    return pl.pallas_call(
        squares_kernel,
        out_shape=jax.ShapeDtypeStruct((8, 128), jnp.float32),
        grid=(1,),
        in_specs=[pl.BlockSpec(value.shape, lambda j: (0, 0)) for value in values],
        out_specs=pl.BlockSpec((8, 128), lambda j: (0, 0)),
        compiler_params=pltpu.CompilerParams(vmem_limit_bytes=12 * 2**20),
        cost_estimate=pl.CostEstimate(flops=2 * size, bytes_accessed=2 * size, transcendentals=0),
    )(*values)


def place_kernel(entries, spots_ref, squares_ref, *refs):
    count = len(entries)
    ins, (down_ref, up_ref), buffers = refs[:count], refs[count : count + 2], refs[count + 2 : -1]
    out_sems = refs[-1]

    def stores(n, kind):
        part, flip_half, _ = entries[n]
        first, width = PARTS[part]
        half = spots_ref[part] ^ flip_half
        copies = []
        for k in range(4):
            start = 4 * first + k * width
            if kind == 0:
                target = down_ref.at[half, k, :, pl.ds(first, width)]
            else:
                target = up_ref.at[half, :, pl.ds(start, width)]
            copies.append(pltpu.make_async_copy(buffers[n].at[k], target, out_sems.at[n, k]))
        return copies

    def each(n, act):
        own_kind = spots_ref[3 + entries[n][0]] ^ entries[n][2]
        for kind in range(2):

            @pl.when(own_kind == kind)
            def _(kind=kind):
                for copy in stores(n, kind):
                    act(copy)

    entries_in_all = jnp.float32(D_IN * RANK + RANK * D_OUT)
    mean_square = jnp.sum(squares_ref[...], keepdims=True) / entries_in_all
    clip = jnp.minimum(jnp.float32(1.0), 1.0 / jnp.sqrt(mean_square + 1e-06))
    for n in range(count):
        for k in range(4):
            buffers[n][k] = (ins[n][k].astype(jnp.float32) * clip).astype(jnp.bfloat16)
        each(n, lambda copy: copy.start())
    for n in range(count):
        each(n, lambda copy: copy.wait())


def place(spots, squares, entries):
    values = [entry[3].reshape(4, 256, PARTS[entry[0]][1]) for entry in entries]
    anywhere = pl.BlockSpec(memory_space=pl.ANY)
    smem = pl.BlockSpec(memory_space=pltpu.SMEM)
    size = sum(1024 * PARTS[entry[0]][1] for entry in entries)
    return pl.pallas_call(
        functools.partial(place_kernel, [entry[:3] for entry in entries]),
        out_shape=(
            jax.ShapeDtypeStruct((2, 4, 256, RANK), jnp.bfloat16),
            jax.ShapeDtypeStruct((2, 256, D_OUT), jnp.bfloat16),
        ),
        in_specs=[smem] + [pl.BlockSpec(memory_space=pltpu.VMEM)] * (1 + len(values)),
        out_specs=(anywhere, anywhere),
        scratch_shapes=[pltpu.VMEM((4, 256, PARTS[entry[0]][1]), jnp.bfloat16) for entry in entries]
        + [pltpu.SemaphoreType.DMA((len(entries), 4))],
        compiler_params=pltpu.CompilerParams(vmem_limit_bytes=20 * 2**20),
        cost_estimate=pl.CostEstimate(flops=size, bytes_accessed=4 * size, transcendentals=0),
    )(spots, squares, *values)


def scatter_four(values, dims, bits, beside):
    rows = values.shape[0] // 4
    me = 2 * bits[dims[0]] + bits[dims[1]]
    own, *sends = [lax.dynamic_slice_in_dim(values, (me ^ flip) * rows, rows) for flip in (0, 3, 2, 1)]
    sends = [send.astype(jnp.bfloat16) for send in sends]
    recvs = beside(sends, lambda sends: [swap(send, dim) for send, dim in zip(sends, (dims, *dims))])
    return own + sum(recv.astype(jnp.float32) for recv in recvs)


def gather_four(block, dims, bits, beside):
    both, first, second = beside(block, lambda block: [swap(block, dim) for dim in (dims, *dims)])
    bit = bits[dims[1]]
    return join(join(block, second, bit), join(first, both, bit), bits[dims[0]])


def join(mine, other, bit):
    return jnp.where(bit == 0, jnp.concatenate([mine, other]), jnp.concatenate([other, mine]))


def fill(mine, other, bit, axis):
    size = mine.shape[axis]
    return lax.dynamic_update_slice_in_dim(jnp.concatenate([mine, mine], axis=axis), other, (1 - bit) * size, axis)


def shards(inputs, out_grad, w_frozen, adapter_down, adapter_up):
    core = lax.axis_index("tensor")
    chip = lax.axis_index("dp")
    bits = ring_bits(chip, core)
    parts = range(3)
    dims = [ORDERS[part] for part in parts]
    b0 = [bits[dims[part][0]] for part in parts]
    b1 = [bits[dims[part][1]] for part in parts]
    b2 = [bits[dims[part][2]] for part in parts]

    out_other = swap(out_grad, "t")
    part_latent = jnp.einsum("dr,td->rt", adapter_down, inputs, preferred_element_type=jnp.float32)
    sent = lax.dynamic_slice_in_dim(part_latent, (1 - core) * 512, 512)
    latent_t = (lax.dynamic_slice_in_dim(part_latent, core * 512, 512) + swap(sent, "t")).astype(jnp.bfloat16)
    piece = fill(out_grad, out_other, core, 0)
    grad_half = jnp.einsum("to,ro->tr", piece, adapter_up, preferred_element_type=jnp.float32).astype(jnp.bfloat16)
    latent_grad = fill(grad_half, swap(grad_half, "t"), core, 1)
    operands = (inputs.T, latent_grad, latent_t, piece)
    spots = jnp.stack(b0 + b1 + b2).astype(jnp.int32)

    pieces = []

    def beside(values, exchange):
        rows = slice(len(pieces) * 512, len(pieces) * 512 + 512)
        values, piece_now, latent_now = lax.optimization_barrier((values, piece, latent_grad))
        part_grad = (
            jnp.einsum("to,io->ti", piece_now, w_frozen[rows], preferred_element_type=jnp.float32)
            + jnp.einsum("tr,dr->td", latent_now, adapter_down[rows], preferred_element_type=jnp.float32)
        ).astype(jnp.bfloat16)
        values, part_grad = lax.optimization_barrier((exchange(values), part_grad))
        pieces.append(part_grad)
        return values

    ahead, behind = [None] * 3, [None] * 3
    for part in (0, 1):
        ahead[part] = swap(grads(spots, operands, part, "ahead"), dims[part][0])
    ahead[2] = behind[2] = swap(grads(spots, operands, 2, "first"), dims[2][0])
    for part in (0, 1):
        ready = grads(spots, operands, part, "behind")
        behind[part] = swap(ready, dims[part][0])
    recvs = []
    for part in parts:
        if part == 2:
            (recv, behind), _ = lax.optimization_barrier(((ahead[part], behind), ready))
        else:
            recv, _ = lax.optimization_barrier((ahead[part], ready))
        ready = grads(spots, operands, part, "second", recv)
        recvs.append(swap(ready, dims[part][1]))
    keeps = [None] * 3

    def keep_own(part):
        kept, _ = lax.optimization_barrier(((behind[part], arrived[part]), ready))
        return grads(spots, operands, part, "own", *kept)

    arrived = [None] * 3
    for part in (1, 0, 2):
        arrived[part], _ = lax.optimization_barrier((recvs[part], ready))
        ready = grads(spots, operands, part, "third", behind[part], arrived[part])
        recvs[part] = swap(ready, dims[part][2])
        if part == 1:
            keeps[part] = keep_own(part)
            ready = keeps[part]
    for part in (0, 2):
        keeps[part] = keep_own(part)

    def side_by_side(values):
        return jnp.concatenate([value.reshape(512, -1) for value in values], axis=1).astype(jnp.float32)

    own = side_by_side(keeps) + side_by_side(recvs)
    own = scatter_four(own, ("x2", "y2"), bits, beside)
    own = scatter_four(own, ("z2", "z4"), bits, beside)
    block = own.astype(jnp.bfloat16)

    block = gather_four(block, ("z2", "z4"), bits, beside)
    block = gather_four(block, ("x2", "y2"), bits, beside)
    mine = [block[:, first : first + width] for first, width in PARTS]
    mine = [fill(mine[part], swap(mine[part], dims[part][2]), b2[part], 0) for part in parts]
    second = [swap(mine[part], dims[part][1]) for part in parts]
    third = [swap(mine[part], dims[part][0]) for part in (0, 1)]
    fourth = [swap(second[part], dims[part][0]) for part in (0, 1)]
    last = swap(jnp.concatenate([mine[2], second[2]]), dims[2][0])

    squares = squares_of(mine + second) + squares_of(third + [last]) + squares_of(fourth)
    squares = squares + swap(squares, "t")
    third.append(last[:1024])
    fourth.append(last[1024:])
    quarters = [
        (part, flip_half, flip_kind, values[part])
        for flip_half, flip_kind, values in ((0, 0, mine), (0, 1, second), (1, 0, third), (1, 1, fourth))
        for part in parts
    ]
    outs = place(spots, squares, quarters)

    input_grad = jnp.concatenate(pieces, axis=1)
    return (input_grad, outs[0].reshape(2048, RANK), outs[1].reshape(512, D_OUT))


def solution(mesh):
    in_specs = (
        P("dp", "tensor"),
        P(("dp", "tensor"), None),
        P("tensor", None),
        P("tensor", None),
        P("tensor", None),
    )
    out_specs = (P("dp", "tensor"), P("tensor", None), P("tensor", None))
    return jax.shard_map(shards, mesh=mesh, in_specs=in_specs, out_specs=out_specs, check_vma=False)
```

```python
import functools

import jax
import jax.numpy as jnp
from jax import lax
from jax.experimental import pallas as pl
from jax.experimental.pallas import tpu as pltpu
from jax.sharding import PartitionSpec as P

D_IN = 4096
D_OUT = 4096
RANK = 1024
NX, NY, NZ = 4, 4, 8

PARTS = ((0, 384), (384, 384), (768, 256))
ORDERS = (("x1", "y1", "z1"), ("y1", "z1", "x1"), ("z1", "x1", "y1"))
TAIL = ("x2", "y2", "z2", "z4")


def ring_bits(chip, core):
    xs = ((chip & (NX - 1)) - core) & (NX - 1)
    ys = (((chip >> 2) & (NY - 1)) - core) & (NY - 1)
    zs = ((chip >> 4) - core) & (NZ - 1)
    return {
        "x1": ((xs + 1) >> 1) & 1,
        "x2": xs >> 1,
        "y1": ((ys + 1) >> 1) & 1,
        "y2": ys >> 1,
        "z1": zs & 1,
        "z2": (zs >> 1) & 1,
        "z4": zs >> 2,
    }


def partner_pairs(dim):
    pairs = []
    for z in range(NZ):
        for y in range(NY):
            for x in range(NX):
                for c in range(2):
                    x2, y2, z2 = x, y, z
                    if dim[0] == "x":
                        xs = (x - c) % NX
                        ps = xs ^ 1 if dim == "x1" else 3 - xs
                        x2 = (ps + c) % NX
                    elif dim[0] == "y":
                        ys = (y - c) % NY
                        ps = ys ^ 1 if dim == "y1" else 3 - ys
                        y2 = (ps + c) % NY
                    elif dim[0] == "z":
                        zs = (z - c) % NZ
                        z2 = ((zs ^ int(dim[1])) + c) % NZ
                    source = ((z * NY + y) * NX + x) * 2 + c
                    target = ((z2 * NY + y2) * NX + x2) * 2 + c
                    pairs.append((source, target))
    return pairs


PAIRS = {dim: partner_pairs(dim) for dim in ("x1", "x2", "y1", "y2", "z1", "z2", "z4")}


def both_pairs(first, second):
    along = dict(PAIRS[second])
    return [(source, along[target]) for source, target in PAIRS[first]]


def swap(value, dim):
    if dim == "t":
        return lax.ppermute(value, "tensor", [(0, 1), (1, 0)])
    if isinstance(dim, tuple):
        return lax.ppermute(value, ("dp", "tensor"), both_pairs(*dim))
    return lax.ppermute(value, ("dp", "tensor"), PAIRS[dim])


def grads_kernel(part, stage, spots_ref, in_ref, lg_ref, lat_ref, og_ref, *refs):
    width = PARTS[part][1]

    def down(k):
        rows = pl.ds(256 * k, 256)
        return jnp.dot(in_ref[rows], lg_ref[...], preferred_element_type=jnp.float32)

    def up(k):
        return jnp.dot(lat_ref[...], og_ref[:, k * width : (k + 1) * width], preferred_element_type=jnp.float32)

    if stage == "first":
        (first_ref,) = refs
        for k in range(4):
            first_ref[0, k] = down(k).astype(jnp.bfloat16)
            first_ref[1, k] = up(k).astype(jnp.bfloat16)
        return

    def run(product):
        for k in range(2 if stage in ("third", "own") else 4):
            total = product(k)
            if stage in ("ahead", "behind"):
                refs[0][k] = total.astype(jnp.bfloat16)
                continue
            total = total + refs[0][0, k].astype(jnp.float32)
            if stage == "second":
                refs[1][k] = total.astype(jnp.bfloat16)
                continue
            refs[2][k] = (total + refs[1][k].astype(jnp.float32)).astype(refs[2].dtype)

    kind = spots_ref[3 + part] ^ (stage in ("ahead", "second"))
    pl.when(kind == 0)(functools.partial(run, down))
    pl.when(kind == 1)(functools.partial(run, up))


def grads(spots, operands, part, stage, *recvs):
    first, width = PARTS[part]
    block = first // width
    other_half = int(stage in ("first", "ahead", "behind"))
    other_kind = int(stage in ("ahead", "second"))
    count = 2 if stage in ("third", "own") else 4

    def piece_of(s):
        return s[6 + part] ^ int(stage == "third") if count == 2 else 0

    pieces = 4 // count
    in_specs = [
        pl.BlockSpec((256 * count, 256), lambda j, s: ((s[part] ^ other_half) * pieces + piece_of(s), 0)),
        pl.BlockSpec((256, width), lambda j, s: (0, block)),
        pl.BlockSpec((256, 256), lambda j, s: (s[part] ^ other_half, 0)),
        pl.BlockSpec((256, count * width), lambda j, s: (0, block * pieces + piece_of(s))),
    ]
    recvs = list(recvs)
    if recvs:
        both = recvs[0].ndim == 4
        recvs[0] = recvs[0].reshape(-1, 4, 256, width)
        in_specs.append(
            pl.BlockSpec(
                (1, count, 256, width), lambda j, s: (s[3 + part] ^ other_kind if both else 0, piece_of(s), 0, 0)
            )
        )
    if count == 2:
        in_specs.append(pl.BlockSpec((2, 256, width), lambda j, s: (piece_of(s), 0, 0)))
    shape = (2, 4, 256, width) if stage == "first" else (count, 256, width)
    dtype = jnp.float32 if stage == "own" else jnp.bfloat16
    products = len(shape) - 2 if stage == "first" else count / 4
    return pl.pallas_call(
        functools.partial(grads_kernel, part, stage),
        out_shape=jax.ShapeDtypeStruct(shape, dtype),
        grid_spec=pltpu.PrefetchScalarGridSpec(
            num_scalar_prefetch=1,
            grid=(1,),
            in_specs=in_specs,
            out_specs=pl.BlockSpec(shape, lambda j, s: (0,) * len(shape)),
        ),
        compiler_params=pltpu.CompilerParams(vmem_limit_bytes=8 * 2**20),
        cost_estimate=pl.CostEstimate(
            flops=int(2 * 1024 * 256 * width * products),
            bytes_accessed=int(2048 * width * products) + 2 * 256 * (1024 + 256 + 5 * width),
            transcendentals=0,
        ),
    )(spots, *operands, *recvs)


def squares_kernel(*refs):
    total = jnp.zeros((8, 128), jnp.float32)
    for ref in refs[:-1]:
        rows, width = ref.shape
        for column in range(0, width, 128):

            def add(step, total, ref=ref, column=column):
                values = ref[pl.ds(pl.multiple_of(step * 128, 128), 128), column : column + 128].astype(jnp.float32)
                return total + jnp.sum((values * values).reshape(16, 8, 128), axis=0)

            total = lax.fori_loop(0, rows // 128, add, total)
    refs[-1][...] = total


def squares_of(values):
    size = sum(value.size for value in values)
    return pl.pallas_call(
        squares_kernel,
        out_shape=jax.ShapeDtypeStruct((8, 128), jnp.float32),
        grid=(1,),
        in_specs=[pl.BlockSpec(value.shape, lambda j: (0, 0)) for value in values],
        out_specs=pl.BlockSpec((8, 128), lambda j: (0, 0)),
        compiler_params=pltpu.CompilerParams(vmem_limit_bytes=12 * 2**20),
        cost_estimate=pl.CostEstimate(flops=2 * size, bytes_accessed=2 * size, transcendentals=0),
    )(*values)


def place_kernel(entries, spots_ref, squares_ref, *refs):
    count = len(entries)
    ins, (down_ref, up_ref), buffers = refs[:count], refs[count : count + 2], refs[count + 2 : -1]
    out_sems = refs[-1]

    def stores(n, kind):
        part, flip_half, _ = entries[n]
        first, width = PARTS[part]
        half = spots_ref[part] ^ flip_half
        copies = []
        for k in range(4):
            start = 4 * first + k * width
            if kind == 0:
                target = down_ref.at[half, k, :, pl.ds(first, width)]
            else:
                target = up_ref.at[half, :, pl.ds(start, width)]
            copies.append(pltpu.make_async_copy(buffers[n].at[k], target, out_sems.at[n, k]))
        return copies

    def each(n, act):
        own_kind = spots_ref[3 + entries[n][0]] ^ entries[n][2]
        for kind in range(2):

            @pl.when(own_kind == kind)
            def _(kind=kind):
                for copy in stores(n, kind):
                    act(copy)

    entries_in_all = jnp.float32(D_IN * RANK + RANK * D_OUT)
    mean_square = jnp.sum(squares_ref[...], keepdims=True) / entries_in_all
    clip = jnp.minimum(jnp.float32(1.0), 1.0 / jnp.sqrt(mean_square + 1e-06))
    for n in range(count):
        for k in range(4):
            buffers[n][k] = (ins[n][k].astype(jnp.float32) * clip).astype(jnp.bfloat16)
        each(n, lambda copy: copy.start())
    for n in range(count):
        each(n, lambda copy: copy.wait())


def place(spots, squares, entries):
    values = [entry[3].reshape(4, 256, PARTS[entry[0]][1]) for entry in entries]
    anywhere = pl.BlockSpec(memory_space=pl.ANY)
    smem = pl.BlockSpec(memory_space=pltpu.SMEM)
    size = sum(1024 * PARTS[entry[0]][1] for entry in entries)
    return pl.pallas_call(
        functools.partial(place_kernel, [entry[:3] for entry in entries]),
        out_shape=(
            jax.ShapeDtypeStruct((2, 4, 256, RANK), jnp.bfloat16),
            jax.ShapeDtypeStruct((2, 256, D_OUT), jnp.bfloat16),
        ),
        in_specs=[smem] + [pl.BlockSpec(memory_space=pltpu.VMEM)] * (1 + len(values)),
        out_specs=(anywhere, anywhere),
        scratch_shapes=[pltpu.VMEM((4, 256, PARTS[entry[0]][1]), jnp.bfloat16) for entry in entries]
        + [pltpu.SemaphoreType.DMA((len(entries), 4))],
        compiler_params=pltpu.CompilerParams(vmem_limit_bytes=20 * 2**20),
        cost_estimate=pl.CostEstimate(flops=size, bytes_accessed=4 * size, transcendentals=0),
    )(spots, squares, *values)


def scatter_four(values, dims, bits, beside):
    rows = values.shape[0] // 4
    me = 2 * bits[dims[0]] + bits[dims[1]]
    own, *sends = [lax.dynamic_slice_in_dim(values, (me ^ flip) * rows, rows) for flip in (0, 3, 2, 1)]
    sends = [send.astype(jnp.bfloat16) for send in sends]
    recvs = beside(sends, lambda sends: [swap(send, dim) for send, dim in zip(sends, (dims, *dims))])
    return own + sum(recv.astype(jnp.float32) for recv in recvs)


def gather_four(block, dims, bits, beside):
    both, first, second = beside(block, lambda block: [swap(block, dim) for dim in (dims, *dims)])
    bit = bits[dims[1]]
    return join(join(block, second, bit), join(first, both, bit), bits[dims[0]])


def join(mine, other, bit):
    return jnp.where(bit == 0, jnp.concatenate([mine, other]), jnp.concatenate([other, mine]))


def fill(mine, other, bit, axis):
    size = mine.shape[axis]
    return lax.dynamic_update_slice_in_dim(jnp.concatenate([mine, mine], axis=axis), other, (1 - bit) * size, axis)


def shards(inputs, out_grad, w_frozen, adapter_down, adapter_up):
    core = lax.axis_index("tensor")
    chip = lax.axis_index("dp")
    bits = ring_bits(chip, core)
    parts = range(3)
    dims = [ORDERS[part] for part in parts]
    b0 = [bits[dims[part][0]] for part in parts]
    b1 = [bits[dims[part][1]] for part in parts]
    b2 = [bits[dims[part][2]] for part in parts]

    out_other = swap(out_grad, "t")
    part_latent = jnp.einsum("dr,td->rt", adapter_down, inputs, preferred_element_type=jnp.float32)
    sent = lax.dynamic_slice_in_dim(part_latent, (1 - core) * 512, 512)
    latent_t = (lax.dynamic_slice_in_dim(part_latent, core * 512, 512) + swap(sent, "t")).astype(jnp.bfloat16)
    piece = fill(out_grad, out_other, core, 0)
    grad_half = jnp.einsum("to,ro->tr", piece, adapter_up, preferred_element_type=jnp.float32).astype(jnp.bfloat16)
    latent_grad = fill(grad_half, swap(grad_half, "t"), core, 1)
    operands = (inputs.T, latent_grad, latent_t, piece)
    spots = jnp.stack(b0 + b1 + b2).astype(jnp.int32)

    pieces = []

    def beside(values, exchange):
        rows = slice(len(pieces) * 512, len(pieces) * 512 + 512)
        values, piece_now, latent_now = lax.optimization_barrier((values, piece, latent_grad))
        part_grad = (
            jnp.einsum("to,io->ti", piece_now, w_frozen[rows], preferred_element_type=jnp.float32)
            + jnp.einsum("tr,dr->td", latent_now, adapter_down[rows], preferred_element_type=jnp.float32)
        ).astype(jnp.bfloat16)
        values, part_grad = lax.optimization_barrier((exchange(values), part_grad))
        pieces.append(part_grad)
        return values

    ahead, behind = [None] * 3, [None] * 3
    for part in (0, 1):
        ahead[part] = swap(grads(spots, operands, part, "ahead"), dims[part][0])
    ahead[2] = behind[2] = swap(grads(spots, operands, 2, "first"), dims[2][0])
    for part in (0, 1):
        ready = grads(spots, operands, part, "behind")
        behind[part] = swap(ready, dims[part][0])
    recvs = []
    for part in parts:
        if part == 2:
            (recv, behind), _ = lax.optimization_barrier(((ahead[part], behind), ready))
        else:
            recv, _ = lax.optimization_barrier((ahead[part], ready))
        ready = grads(spots, operands, part, "second", recv)
        recvs.append(swap(ready, dims[part][1]))
    keeps = [None] * 3

    def keep_own(part):
        kept, _ = lax.optimization_barrier(((behind[part], arrived[part]), ready))
        return grads(spots, operands, part, "own", *kept)

    arrived = [None] * 3
    for part in (1, 0, 2):
        arrived[part], _ = lax.optimization_barrier((recvs[part], ready))
        ready = grads(spots, operands, part, "third", behind[part], arrived[part])
        recvs[part] = swap(ready, dims[part][2])
        if part == 1:
            keeps[part] = keep_own(part)
            ready = keeps[part]
    for part in (0, 2):
        keeps[part] = keep_own(part)

    def side_by_side(values):
        return jnp.concatenate([value.reshape(512, -1) for value in values], axis=1).astype(jnp.float32)

    own = side_by_side(keeps) + side_by_side(recvs)
    own = scatter_four(own, ("x2", "y2"), bits, beside)
    own = scatter_four(own, ("z2", "z4"), bits, beside)
    block = own.astype(jnp.bfloat16)

    block = gather_four(block, ("z2", "z4"), bits, beside)
    block = gather_four(block, ("x2", "y2"), bits, beside)
    mine = [block[:, first : first + width] for first, width in PARTS]
    mine = [fill(mine[part], swap(mine[part], dims[part][2]), b2[part], 0) for part in parts]
    second = [swap(mine[part], dims[part][1]) for part in parts]
    third = [swap(mine[part], dims[part][0]) for part in (0, 1)]
    fourth = [swap(second[part], dims[part][0]) for part in (0, 1)]
    last = swap(jnp.concatenate([mine[2], second[2]]), dims[2][0])

    squares = squares_of(mine + second) + squares_of(third + [last]) + squares_of(fourth)
    squares = squares + swap(squares, "t")
    third.append(last[:1024])
    fourth.append(last[1024:])
    quarters = [
        (part, flip_half, flip_kind, values[part])
        for flip_half, flip_kind, values in ((0, 0, mine), (0, 1, second), (1, 0, third), (1, 1, fourth))
        for part in parts
    ]
    outs = place(spots, squares, quarters)

    input_grad = jnp.concatenate(pieces, axis=1)
    return (input_grad, outs[0].reshape(2048, RANK), outs[1].reshape(512, D_OUT))


def solution(mesh):
    in_specs = (
        P("dp", "tensor"),
        P(("dp", "tensor"), None),
        P("tensor", None),
        P("tensor", None),
        P("tensor", None),
    )
    out_specs = (P("dp", "tensor"), P("tensor", None), P("tensor", None))
    return jax.shard_map(shards, mesh=mesh, in_specs=in_specs, out_specs=out_specs, check_vma=False)
```
